32 devices in a mesh: gx: 4 (over y, x), gy: 8 (over z, core).
Axes of the slice: x: 2, y: 2, z: 4, core: 2. Of those that a mesh axis runs over, the one named last changes fastest.
Arguments:
- scalar_field: float32 [64, 256, 1024], P(None, 'gy', 'gx'), may hold values from -6 to 6
- velocity: bfloat16 [3, 64, 256, 1024], P(None, None, 'gy', 'gx'), may hold values from -4 to 4
- shear_offset: int32 [2], replicated, may hold values from 0 to 1023
- part_temp: float32 [32, 32, 64], P(('gx', 'gy')), may hold values from -6 to 6
- part_coef: float32 [32, 32, 64], P(('gx', 'gy')), may hold values from 0.5 to 4
- part_heat: float32 [32, 32, 64], P(('gx', 'gy')), may hold values from 0.2 to 2
- part_cell: int32 [32, 32, 64], P(('gx', 'gy')), may hold values from 0 to 524287
- part_count: int32 [32, 32], P(('gx', 'gy')), may hold values from 0 to 64, as said below
Outputs:
- scalar_out: float32 [64, 256, 1024], P(None, 'gy', 'gx')
- temp_out: float32 [32, 32, 64], P(('gx', 'gy'))
The draws below stay inside these ranges and needn't reach their ends.
Inputs may be any that keep to these rules, and one draw needn't show every extreme that they name: Slots below part_count[s, d] are live; in every draw one owning device receives 64 live slots from every holding device, and another receives none.
All inputs are finite; a program needn't handle non-finite values.
Results may differ from the reference program's by a relative error of at most 0.0003.
Values sent between devices are 32-bit elements; how exact they have to be, the bound alone decides.
A program may use at most 64 MiB of HBM per device.

```python
import math
import jax
import jax.numpy as jnp
from jax import lax

CX = 256
CY = 32
NZ = 64
CAP = 64
NX = 1024
NY = 256
PEERS = 32
N_GY = 8


def draw_part_count(key, part):
    first, second, third, fourth = jax.random.split(key, 4)
    dest_load = jax.random.randint(first, (PEERS,), CAP // 4, CAP + 1)
    counts = jax.random.randint(second, (PEERS, PEERS), (dest_load // 2)[None, :], dest_load[None, :] + 1)
    hot_dest = jax.random.randint(third, (), 0, PEERS)
    cold_dest = (hot_dest + 1 + jax.random.randint(fourth, (), 0, PEERS - 1)) % PEERS
    columns = jnp.arange(PEERS)[None, :]
    counts = jnp.where(columns == cold_dest, 0, counts)
    return jnp.where(columns == hot_dest, CAP, counts).astype(jnp.int32)


def plant(entries, rng, low, high):
    dims = entries.shape
    index_at = [jax.random.randint(jax.random.fold_in(rng, axis), (), 0, dims[axis]) for axis in range(len(dims))]
    entries = entries.at[tuple(index_at)].set(low)
    longest = dims.index(max(dims))
    index_at[longest] = (index_at[longest] + 1) % dims[longest]
    return entries.at[tuple(index_at)].set(high)


def level_of(rng, extent, cuts, least, high):
    loudness, own = 1.0, jax.random.fold_in(rng, 6)
    for dim, shards_of in cuts:
        draws = jnp.exp(jax.random.uniform(jax.random.fold_in(own, dim), (shards_of,), jnp.float32, least / len(cuts), high / len(cuts)))
        loudness = loudness * jnp.repeat(draws, extent[dim] // shards_of).reshape([-1 if axis == dim else 1 for axis in range(len(extent))])
    return loudness


def scatter_about(rng, extent, width, reach, shards=(), held_as=jnp.bfloat16):
    level = level_of(rng, extent, shards, -0.22, 0.18) if shards else 1.0
    drawn = jax.random.normal(rng, extent, jnp.float32) * width * level
    return jnp.minimum(jnp.maximum(drawn, -reach), reach).astype(held_as)


def setup_inputs(seed: int = 0) -> dict:
    keys = jax.random.split(jax.random.key(seed), 9)
    return {
        "scalar_field": scatter_about(keys[0], (NZ, NY, NX), 1.0, 6.0, ((1, 8), (2, 4)), jnp.float32),
        "velocity": scatter_about(keys[1], (3, NZ, NY, NX), 0.7, 4.0, ((2, 8), (3, 4))),
        "shear_offset": jax.random.randint(keys[2], (2,), 0, NX).astype(jnp.int32),
        "part_temp": scatter_about(keys[3], (PEERS, PEERS, CAP), 1.0, 6.0, ((0, 32),), jnp.float32),
        "part_coef": jnp.clip(jnp.exp(math.log(4.0) - 2.0794415 * jax.random.uniform(keys[4], (PEERS, PEERS, CAP), jnp.float32) ** level_of(keys[4], (PEERS, PEERS, CAP), ((0, 32),), -0.2, 0.2)), 0.5, 4.0),
        "part_heat": jnp.clip(jnp.exp(math.log(2.0) - 2.3025851 * jax.random.uniform(keys[5], (PEERS, PEERS, CAP), jnp.float32) ** level_of(keys[5], (PEERS, PEERS, CAP), ((0, 32),), -0.2, 0.2)), 0.2, 2.0),
        "part_cell": plant(jax.random.randint(keys[6], (PEERS, PEERS, CAP), 0, NZ * CY * CX), jax.random.fold_in(keys[6], 1), 0, (NZ * CY * CX) - 1).astype(jnp.int32),
        "part_count": draw_part_count(jax.random.fold_in(keys[8], 71), 0),
    }


time_step = 0.1
diffusivity = 0.1
mean_speed = 1.0
mean_gradient = 1.0
heat_share = 0.5


def derivative(extended, axis, length):
    minus_two = lax.slice_in_dim(extended, 0, length, axis=axis)
    minus_one = lax.slice_in_dim(extended, 1, length + 1, axis=axis)
    center = lax.slice_in_dim(extended, 2, length + 2, axis=axis)
    plus_one = lax.slice_in_dim(extended, 3, length + 3, axis=axis)
    plus_two = lax.slice_in_dim(extended, 4, length + 4, axis=axis)
    grad = (8.0 * (plus_one - minus_one) - (plus_two - minus_two)) / 12.0
    lap = (16.0 * (plus_one + minus_one) - (plus_two + minus_two) - 30.0 * center) / 12.0
    return grad, lap


def tendency(center, x_extended, y_extended, z_extended, velocity, mean_flow, source):
    grad_x, lap_x = derivative(x_extended, 2, center.shape[2])
    grad_y, lap_y = derivative(y_extended, 1, center.shape[1])
    grad_z, lap_z = derivative(z_extended, 0, center.shape[0])
    along_x = velocity[0].astype(jnp.float32)
    along_y = velocity[1].astype(jnp.float32)
    along_z = velocity[2].astype(jnp.float32)
    return (-(along_x + mean_flow) * grad_x - along_y * grad_y - along_z * grad_z
            - mean_gradient * along_y + diffusivity * (lap_x + lap_y + lap_z) + heat_share * source)


def reference(scalar_field, velocity, shear_offset, part_temp, part_coef, part_heat, part_cell, part_count):
    slots = jnp.arange(CAP).astype(jnp.int32)
    live_slot = slots[None, None, :] < part_count[:, :, None]
    live_coef = jnp.where(live_slot, part_coef, jnp.float32(0.0))
    owners = jnp.arange(PEERS).astype(jnp.int32)
    owner_x = (owners // N_GY)[None, :, None]
    owner_y = (owners % N_GY)[None, :, None]
    plane_at = part_cell // (CY * CX)
    row_at = (part_cell // CX) % CY
    col_at = part_cell % CX
    global_cell = (plane_at * (NY * NX) + (owner_y * CY + row_at) * NX + owner_x * CX + col_at).astype(jnp.int32)
    flat_cells = global_cell.reshape(-1)
    rows_y = jnp.arange(NY).astype(jnp.float32)
    mean_flow = (mean_speed * (2.0 * (rows_y + 0.5) / NY - 1.0))[:, None]

    def sample_at(field):
        return field.reshape(-1)[global_cell]

    def field_rhs(field, offset, flux):
        source = jnp.zeros(NZ * NY * NX, jnp.float32).at[flat_cells].add(flux.reshape(-1)).reshape(NZ, NY, NX)
        z_padded = jnp.concatenate([field[-2:], field, field[:2]], axis=0)

        def one_plane(plane):
            window = lax.dynamic_slice_in_dim(z_padded, plane, 5, 0)
            center = window[2:3]
            x_extended = jnp.concatenate([center[:, :, -2:], center, center[:, :, :2]], axis=2)
            upper = jnp.roll(center[:, :2], offset, axis=2)
            lower = jnp.roll(center[:, -2:], -offset, axis=2)
            y_extended = jnp.concatenate([lower, center, upper], axis=1)
            vel_plane = lax.dynamic_slice_in_dim(velocity, plane, 1, 1)
            source_plane = lax.dynamic_slice_in_dim(source, plane, 1, 0)
            return tendency(center, x_extended, y_extended, window, vel_plane, mean_flow, source_plane)[0]

        return lax.map(one_plane, jnp.arange(NZ).astype(jnp.int32))

    flux_one = live_coef * (part_temp - sample_at(scalar_field))
    section_one = scalar_field + time_step * field_rhs(scalar_field, shear_offset[0], flux_one)
    temp_one = part_temp + time_step * (part_heat - flux_one)
    flux_two = live_coef * (temp_one - sample_at(section_one))
    scalar_out = 0.75 * scalar_field + 0.25 * (section_one + time_step * field_rhs(section_one, shear_offset[1], flux_two))
    temp_two = 0.75 * part_temp + 0.25 * (temp_one + time_step * (part_heat - flux_two))
    temp_out = jnp.where(live_slot, temp_two, jnp.float32(0.0))
    return scalar_out, temp_out
```

```python
import functools

import jax
import jax.numpy as jnp
from jax import lax
from jax.experimental import pallas as pl
from jax.experimental.pallas import tpu as pltpu
from jax.sharding import PartitionSpec as P

time_step = 0.1
diffusivity = 0.1
mean_speed = 1.0
mean_gradient = 1.0
heat_share = 0.5

MESH = pl.DeviceIdType.MESH
MIB = 1 << 20
BLOCK = 128
WAYS = 4


def halo_kernel(gx_count, gy_count, e_right, e_left, lo, hi, o_left, o_right, y_up, y_low,
                send_x, recv_x, send_lo, recv_up, send_hi, recv_low):
    gx = lax.axis_index("gx")
    gy = lax.axis_index("gy")
    right = lax.rem(gx + 1, gx_count)
    left = lax.rem(gx + gx_count - 1, gx_count)
    first = gy == 0
    last = gy == gy_count - 1

    barrier = pltpu.get_barrier_semaphore()

    def greet(x, y):
        pl.semaphore_signal(barrier, inc=1, device_id=(x, y), device_id_type=MESH)

    greet(right, gy)
    greet(left, gy)

    @pl.when(jnp.logical_not(first))
    def _():
        greet(gx, gy - 1)

    @pl.when(jnp.logical_not(last))
    def _():
        greet(gx, gy + 1)

    @pl.when(first)
    def _():
        for g in range(gx_count):
            greet(g, gy_count - 1)

    @pl.when(last)
    def _():
        for g in range(gx_count):
            greet(g, 0)

    edge = jnp.logical_or(first, last)

    @pl.when(edge)
    def _():
        pl.semaphore_wait(barrier, 3 + gx_count)

    @pl.when(jnp.logical_not(edge))
    def _():
        pl.semaphore_wait(barrier, 4)

    def copy_x(src, dst, k, x):
        return pltpu.make_async_remote_copy(
            src_ref=src, dst_ref=dst, send_sem=send_x.at[k], recv_sem=recv_x.at[k],
            device_id=(x, gy), device_id_type=MESH)

    def copy_lo(g, x, y):
        return pltpu.make_async_remote_copy(
            src_ref=lo, dst_ref=y_up.at[gx], send_sem=send_lo.at[g], recv_sem=recv_up.at[gx],
            device_id=(x, y), device_id_type=MESH)

    def copy_hi(g, x, y):
        return pltpu.make_async_remote_copy(
            src_ref=hi, dst_ref=y_low.at[gx], send_sem=send_hi.at[g], recv_sem=recv_low.at[gx],
            device_id=(x, y), device_id_type=MESH)

    def all_copies(act):
        @pl.when(first)
        def _():
            for g in range(gx_count):
                act(copy_lo(g, g, gy_count - 1))

        @pl.when(last)
        def _():
            for g in range(gx_count):
                act(copy_hi(g, g, 0))

        @pl.when(jnp.logical_not(first))
        def _():
            act(copy_lo(0, gx, gy - 1))

        @pl.when(jnp.logical_not(last))
        def _():
            act(copy_hi(0, gx, gy + 1))

    all_copies(lambda c: c.start())
    to_right = copy_x(e_right, o_left, 0, right)
    to_left = copy_x(e_left, o_right, 1, left)
    to_right.start()
    to_left.start()

    def arrive(rows, slots, sems, s):
        pltpu.make_async_remote_copy(
            src_ref=rows, dst_ref=slots.at[s], send_sem=send_lo.at[0], recv_sem=sems.at[s],
            device_id=(right, gy), device_id_type=MESH).wait_recv()

    @pl.when(last)
    def _():
        for s in range(gx_count):
            arrive(lo, y_up, recv_up, s)

    @pl.when(jnp.logical_not(last))
    def _():
        arrive(lo, y_up, recv_up, gx)

    @pl.when(first)
    def _():
        for s in range(gx_count):
            arrive(hi, y_low, recv_low, s)

    @pl.when(jnp.logical_not(first))
    def _():
        arrive(hi, y_low, recv_low, gx)

    to_right.wait_recv()
    to_left.wait_recv()
    all_copies(lambda c: c.wait_send())
    to_right.wait_send()
    to_left.wait_send()


def halo(which, gx_count, gy_count, e_right, e_left, lo, hi):
    anyspace = pl.BlockSpec(memory_space=pl.ANY)
    sem = pltpu.SemaphoreType.DMA
    f32 = jnp.float32
    return pl.pallas_call(
        functools.partial(halo_kernel, gx_count, gy_count),
        out_shape=[
            jax.ShapeDtypeStruct(e_right.shape, f32),
            jax.ShapeDtypeStruct(e_left.shape, f32),
            jax.ShapeDtypeStruct((gx_count,) + lo.shape, f32),
            jax.ShapeDtypeStruct((gx_count,) + hi.shape, f32),
        ],
        in_specs=[anyspace] * 4,
        out_specs=[anyspace] * 4,
        scratch_shapes=[sem((2,)), sem((2,))] + [sem((gx_count,))] * 4,
        compiler_params=pltpu.CompilerParams(collective_id=which, has_side_effects=True),
        name="halo_%d" % which,
    )(e_right, e_left, lo, hi)


def stencil_kernel(second, dims, full_y, *refs):
    nz, cy, cx = dims
    if second:
        f, vel, o_left, o_right, y_up, y_low, info, f0, q2, out, xe, yg, ring = refs
    else:
        f, vel, o_left, o_right, y_up, y_low, info, out, xe, yg, ring = refs
    gx_count = y_up.shape[0]
    k8 = lax.broadcasted_iota(jnp.int32, (8, 128), 0)
    l8 = lax.broadcasted_iota(jnp.int32, (8, 128), 1)
    hot = ((k8 == 0) & (l8 == 126)) | ((k8 == 1) & (l8 == 127)) | ((k8 == 2) & (l8 == 0)) | ((k8 == 3) & (l8 == 1))
    place = jnp.where(hot, 1.0, 0.0).astype(jnp.float32)
    edges = jnp.concatenate(
        [o_left[...], o_right[...], jnp.zeros((4, nz * cy), jnp.float32)], axis=0)
    xe[...] = lax.dot_general(
        edges, place, (((0,), (0,)), ((), ())), precision=lax.Precision.HIGHEST,
        preferred_element_type=jnp.float32)

    lane = lax.broadcasted_iota(jnp.int32, (nz, cx), 1)
    for src, q_at, base in ((y_up, 0, 0), (y_low, 2, 2)):
        q = info[q_at]
        rem = info[q_at + 1]
        nxt = lax.rem(q + 1, gx_count)
        turn = lax.rem(cx - rem, cx)
        for row in range(2):
            a = pltpu.roll(src[q, row], turn, 1)
            b = pltpu.roll(src[nxt, row], turn, 1)
            yg[base + row] = jnp.where(lane < cx - rem, a, b)

    start = (info[4] * cy).astype(jnp.float32)
    rows = lax.broadcasted_iota(jnp.int32, (cy, cx), 0).astype(jnp.float32) + start
    mean_flow = mean_speed * (2.0 * (rows + 0.5) * (1.0 / full_y) - 1.0)
    c8 = 8.0 / 12.0
    c1 = 1.0 / 12.0
    d16 = diffusivity * 16.0 / 12.0
    d1 = diffusivity / 12.0
    d30 = diffusivity * 90.0 / 12.0

    def plane(z, carry):
        c = f[z]
        zm2 = f[lax.rem(z + nz - 2, nz)]
        zm1 = f[lax.rem(z + nz - 1, nz)]
        zp1 = f[lax.rem(z + 1, nz)]
        zp2 = f[lax.rem(z + 2, nz)]
        ring[0:cy] = c
        ring[cy:cy + 1] = yg[0, pl.ds(z, 1)]
        ring[cy + 1:cy + 2] = yg[1, pl.ds(z, 1)]
        ring[cy + 6:cy + 7] = yg[2, pl.ds(z, 1)]
        ring[cy + 7:cy + 8] = yg[3, pl.ds(z, 1)]
        ry = ring[...]
        ym2 = pltpu.roll(ry, 2, 0)[:cy]
        ym1 = pltpu.roll(ry, 1, 0)[:cy]
        yp1 = pltpu.roll(ry, cy + 7, 0)[:cy]
        yp2 = pltpu.roll(ry, cy + 6, 0)[:cy]
        rx = jnp.concatenate([c, xe[pl.ds(pl.multiple_of(z * cy, cy), cy)]], axis=1)
        wide = cx + 128
        xm2 = pltpu.roll(rx, 2, 1)[:, :cx]
        xm1 = pltpu.roll(rx, 1, 1)[:, :cx]
        xp1 = pltpu.roll(rx, wide - 1, 1)[:, :cx]
        xp2 = pltpu.roll(rx, wide - 2, 1)[:, :cx]
        u = vel[0, z].astype(jnp.float32) + mean_flow
        v = vel[1, z].astype(jnp.float32)
        w = vel[2, z].astype(jnp.float32)
        gx_ = c8 * (xp1 - xm1) - c1 * (xp2 - xm2)
        gy_ = c8 * (yp1 - ym1) - c1 * (yp2 - ym2)
        gz_ = c8 * (zp1 - zm1) - c1 * (zp2 - zm2)
        near = ((xp1 + xm1) + (yp1 + ym1)) + (zp1 + zm1)
        far = ((xp2 + xm2) + (yp2 + ym2)) + (zp2 + zm2)
        rhs = (d16 * near - d1 * far - d30 * c) - u * gx_ - v * (gy_ + mean_gradient) - w * gz_
        euler = c + time_step * rhs
        if second:
            out[z] = 0.75 * f0[z] + 0.25 * euler + q2[pl.ds(pl.multiple_of(z * cy, cy), cy)]
        else:
            out[z] = euler
        return carry

    lax.fori_loop(0, nz, plane, 0, unroll=2)


def stencil(second, full_y, f, vel, o_left, o_right, y_up, y_low, info, *more):
    nz, cy, cx = f.shape
    vm = pl.BlockSpec(memory_space=pltpu.VMEM)
    return pl.pallas_call(
        functools.partial(stencil_kernel, second, (nz, cy, cx), full_y),
        out_shape=jax.ShapeDtypeStruct((nz, cy, cx), jnp.float32),
        in_specs=[vm] * 6 + [pl.BlockSpec(memory_space=pltpu.SMEM)] + [vm] * len(more),
        out_specs=vm,
        scratch_shapes=[
            pltpu.VMEM((nz * cy, 128), jnp.float32),
            pltpu.VMEM((4, nz, cx), jnp.float32),
            pltpu.VMEM((cy + 8, cx), jnp.float32),
        ],
        compiler_params=pltpu.CompilerParams(vmem_limit_bytes=32 * MIB),
        cost_estimate=pl.CostEstimate(flops=70 * nz * cy * cx, bytes_accessed=10 * MIB, transcendentals=0),
        name="stencil_two" if second else "stencil_one",
    )(f, vel, o_left, o_right, y_up, y_low, info, *more)


def particle_kernel(second, dims, *refs):
    nz, cy, cx = dims
    if second:
        rows, pack, field, out, packed, buf, acc1, acc2, acc3 = refs
        scale = 0.25 * time_step * heat_share
    else:
        rows, pack, field, base, out, packed, e_right, e_left, lo, hi, buf, acc1, acc2, acc3 = refs
        scale = time_step * heat_share
    accs = (out, acc1, acc2, acc3)
    cells = nz * cy
    blocks = pack.shape[1] // BLOCK

    def clear(i, carry):
        at = pl.ds(pl.multiple_of(i * 64, 64), 64)
        zero = jnp.zeros((64, cx), jnp.float32)
        out[at] = zero if second else base[at]
        for acc in accs[1:]:
            acc[at] = zero
        return carry

    lax.fori_loop(0, cells // 64, clear, 0)
    lane = lax.broadcasted_iota(jnp.int32, (BLOCK, cx), 1)
    lane8 = lax.broadcasted_iota(jnp.int32, (BLOCK, 8), 1)

    def block(b, carry):
        at = pl.multiple_of(b * BLOCK, BLOCK)
        for i in range(BLOCK):
            buf[i:i + 1] = field[pl.ds(rows[at + i], 1)]
        t = pack[:, pl.ds(at, BLOCK)].T
        hit = lane == t[:, 0:1].astype(jnp.int32)
        sample = jnp.sum(jnp.where(hit, buf[...], 0.0), axis=1, keepdims=True)
        now = t[:, 4:5]
        flux = t[:, 2:3] * (now - sample)
        nxt = now + time_step * (t[:, 3:4] - flux)
        if second:
            nxt = 0.75 * t[:, 1:2] + 0.25 * nxt
        packed[:, pl.ds(at, BLOCK)] = jnp.where(lane8 == 4, nxt, t).T
        buf[...] = jnp.where(hit, scale * flux, 0.0)
        for i in range(0, BLOCK, WAYS):
            ats = [pl.ds(rows[at + i + k], 1) for k in range(WAYS)]
            new = [accs[k][ats[k]] + buf[i + k:i + k + 1] for k in range(WAYS)]
            for k in range(WAYS):
                accs[k][ats[k]] = new[k]
        return carry

    lax.fori_loop(0, blocks, block, 0)

    if second:
        def total(i, carry):
            at = pl.ds(pl.multiple_of(i * 64, 64), 64)
            out[at] = (out[at] + acc1[at]) + (acc2[at] + acc3[at])
            return carry

        lax.fori_loop(0, cells // 64, total, 0)
    else:
        lanes = lax.broadcasted_iota(jnp.int32, (128, 128), 1)

        def total(i, carry):
            at = pl.ds(pl.multiple_of(i * 128, 128), 128)
            new = (out[at] + acc1[at]) + (acc2[at] + acc3[at])
            out[at] = new
            ends = pltpu.roll(jnp.where(lanes < 64, new[:, :128], new[:, cx - 128:]), 2, 1).T
            e_right[:, at] = ends[0:2]
            e_left[:, at] = ends[2:4]
            for k in range(128 // cy):
                z = i * (128 // cy) + k
                for row in range(2):
                    lo[row, pl.ds(z, 1)] = new[k * cy + row:k * cy + row + 1]
                    hi[row, pl.ds(z, 1)] = new[k * cy + cy - 2 + row:k * cy + cy - 1 + row]
            return carry

        lax.fori_loop(0, cells // 128, total, 0)


def particles(second, dims, rows, pack, field, *base):
    nz, cy, cx = dims
    f32 = jnp.float32
    vm = pl.BlockSpec(memory_space=pltpu.VMEM)
    outs = [
        jax.ShapeDtypeStruct((nz * cy, cx), f32),
        jax.ShapeDtypeStruct(pack.shape, f32),
    ]
    if not second:
        outs += [jax.ShapeDtypeStruct((2, nz * cy), f32)] * 2
        outs += [jax.ShapeDtypeStruct((2, nz, cx), f32)] * 2
    grid_space = pltpu.VMEM((nz * cy, cx), f32)
    return pl.pallas_call(
        functools.partial(particle_kernel, second, dims),
        out_shape=outs,
        in_specs=[pl.BlockSpec(memory_space=pltpu.SMEM)] + [vm] * (2 + len(base)),
        out_specs=[vm] * len(outs),
        scratch_shapes=[pltpu.VMEM((BLOCK, cx), f32), grid_space, grid_space, grid_space],
        compiler_params=pltpu.CompilerParams(vmem_limit_bytes=32 * MIB),
        cost_estimate=pl.CostEstimate(flops=20 * MIB, bytes_accessed=10 * MIB, transcendentals=0),
        name="particles_two" if second else "particles_one",
    )(rows, pack, field, *base)


def on_device(
    scalar_field, velocity, shear_offset, part_temp, part_coef, part_heat, part_cell, part_count
):
    nz, cy, cx = scalar_field.shape
    cap = part_temp.shape[2]
    gx_index = lax.axis_index("gx")
    gy_index = lax.axis_index("gy")
    gx_count = lax.axis_size("gx")
    gy_count = lax.axis_size("gy")
    peers = gx_count * gy_count
    full_x = cx * gx_count
    full_y = cy * gy_count
    both = ("gx", "gy")
    live_slot = jnp.arange(cap)[None, None, :] < part_count[:, :, None]
    live_coef = jnp.where(live_slot, part_coef, jnp.float32(0.0))

    send = jnp.concatenate(
        [part_cell.astype(jnp.float32)[0], part_temp[0], live_coef[0], part_heat[0]], axis=1)
    came = lax.all_to_all(send, both, split_axis=0, concat_axis=0, tiled=True)
    came = came.reshape(peers, 4, cap).transpose(1, 0, 2).reshape(4, peers * cap)
    cells = came[0].astype(jnp.int32)
    rows = cells // cx
    pack = jnp.concatenate(
        [(cells % cx).astype(jnp.float32)[None], came[1:], came[1:2],
         jnp.zeros((3, peers * cap), jnp.float32)], axis=0)

    def info(offset):
        low_shift = jnp.where(gy_index == 0, (full_x - offset) % full_x, 0)
        high_shift = jnp.where(gy_index == gy_count - 1, offset, 0)
        up = (gx_index * cx - high_shift) % full_x
        low = (gx_index * cx - low_shift) % full_x
        return jnp.stack([up // cx, up % cx, low // cx, low % cx, gy_index]).astype(jnp.int32)

    def ends(field, at):
        return field[:, :, at:at + 2].reshape(nz * cy, 2).T

    halos = halo(
        0, gx_count, gy_count, ends(scalar_field, cx - 2), ends(scalar_field, 0),
        scalar_field[:, :2].transpose(1, 0, 2), scalar_field[:, cy - 2:].transpose(1, 0, 2))
    base = stencil(False, full_y, scalar_field, velocity, *halos, info(shear_offset[0]))
    flat = (nz * cy, cx)
    dims = (nz, cy, cx)
    section_one, pack, e_right, e_left, lo, hi = particles(
        False, dims, rows, pack, scalar_field.reshape(flat), base.reshape(flat))
    halos = halo(1, gx_count, gy_count, e_right, e_left, lo, hi)
    source, pack = particles(True, dims, rows, pack, section_one)
    home = lax.all_to_all(pack[4].reshape(peers, cap), both, split_axis=0, concat_axis=0, tiled=True)
    scalar_out = stencil(
        True, full_y, section_one.reshape(dims), velocity, *halos, info(shear_offset[1]),
        scalar_field, source)
    temp_out = jnp.where(live_slot, home[None], jnp.float32(0.0))
    return (scalar_out, temp_out)


def solution(mesh):
    in_specs = (
        P(None, "gy", "gx"),
        P(None, None, "gy", "gx"),
        P(),
        P(("gx", "gy"), None, None),
        P(("gx", "gy"), None, None),
        P(("gx", "gy"), None, None),
        P(("gx", "gy"), None, None),
        P(("gx", "gy"), None),
    )
    out_specs = (P(None, "gy", "gx"), P(("gx", "gy"), None, None))
    return jax.shard_map(
        on_device, mesh=mesh, in_specs=in_specs, out_specs=out_specs, check_vma=False
    )
```

```python
import functools

import jax
import jax.numpy as jnp
from jax import lax
from jax.experimental import pallas as pl
from jax.experimental.pallas import tpu as pltpu
from jax.sharding import PartitionSpec as P

time_step = 0.1
diffusivity = 0.1
mean_speed = 1.0
mean_gradient = 1.0
heat_share = 0.5

MESH = pl.DeviceIdType.MESH
MIB = 1 << 20
GROUP = 4
LANES = 128
WAYS = 4


def exchange_kernel(gx_count, gy_count, e_right, e_left, lo, hi, mail, o_left, o_right, y_up, y_low, came,
                    send_x, recv_x, send_lo, recv_up, send_hi, recv_low, send_p, recv_p, own_sem):
    gx = lax.axis_index("gx")
    gy = lax.axis_index("gy")
    right = lax.rem(gx + 1, gx_count)
    left = lax.rem(gx + gx_count - 1, gx_count)
    first = gy == 0
    last = gy == gy_count - 1

    barrier = pltpu.get_barrier_semaphore()

    peers = gx_count * gy_count
    me = gx * gy_count + gy

    def peer(i):
        d = lax.rem(me + i, peers)
        return d, (d // gy_count, lax.rem(d, gy_count))

    def greet(i, carry):
        pl.semaphore_signal(barrier, inc=1, device_id=peer(i)[1], device_id_type=MESH)
        return carry

    lax.fori_loop(1, peers, greet, 0)
    own = pltpu.make_async_copy(mail.at[me], came.at[me], own_sem)
    own.start()
    pl.semaphore_wait(barrier, peers - 1)

    def copy_mail(i):
        d, place = peer(i)
        return pltpu.make_async_remote_copy(
            src_ref=mail.at[d], dst_ref=came.at[me], send_sem=send_p.at[d], recv_sem=recv_p.at[me],
            device_id=place, device_id_type=MESH)

    def copy_x(src, dst, k, x):
        return pltpu.make_async_remote_copy(
            src_ref=src, dst_ref=dst, send_sem=send_x.at[k], recv_sem=recv_x.at[k],
            device_id=(x, gy), device_id_type=MESH)

    def copy_lo(g, x, y):
        return pltpu.make_async_remote_copy(
            src_ref=lo, dst_ref=y_up.at[gx], send_sem=send_lo.at[g], recv_sem=recv_up.at[gx],
            device_id=(x, y), device_id_type=MESH)

    def copy_hi(g, x, y):
        return pltpu.make_async_remote_copy(
            src_ref=hi, dst_ref=y_low.at[gx], send_sem=send_hi.at[g], recv_sem=recv_low.at[gx],
            device_id=(x, y), device_id_type=MESH)

    def all_copies(act):
        @pl.when(first)
        def _():
            for g in range(gx_count):
                act(copy_lo(g, g, gy_count - 1))

        @pl.when(last)
        def _():
            for g in range(gx_count):
                act(copy_hi(g, g, 0))

        @pl.when(jnp.logical_not(first))
        def _():
            act(copy_lo(0, gx, gy - 1))

        @pl.when(jnp.logical_not(last))
        def _():
            act(copy_hi(0, gx, gy + 1))

    all_copies(lambda c: c.start())
    to_right = copy_x(e_right, o_left, 0, right)
    to_left = copy_x(e_left, o_right, 1, left)
    to_right.start()
    to_left.start()

    def post(i, carry):
        copy_mail(i).start()
        return carry

    lax.fori_loop(1, peers, post, 0)

    def arrive(rows, slots, sems, s):
        pltpu.make_async_remote_copy(
            src_ref=rows, dst_ref=slots.at[s], send_sem=send_lo.at[0], recv_sem=sems.at[s],
            device_id=(right, gy), device_id_type=MESH).wait_recv()

    @pl.when(last)
    def _():
        for s in range(gx_count):
            arrive(lo, y_up, recv_up, s)

    @pl.when(jnp.logical_not(last))
    def _():
        arrive(lo, y_up, recv_up, gx)

    @pl.when(first)
    def _():
        for s in range(gx_count):
            arrive(hi, y_low, recv_low, s)

    @pl.when(jnp.logical_not(first))
    def _():
        arrive(hi, y_low, recv_low, gx)

    to_right.wait_recv()
    to_left.wait_recv()
    all_copies(lambda c: c.wait_send())
    to_right.wait_send()
    to_left.wait_send()

    def finish(i, carry):
        d, place = peer(i)
        copy = pltpu.make_async_remote_copy(
            src_ref=mail.at[d], dst_ref=came.at[d], send_sem=send_p.at[d], recv_sem=recv_p.at[d],
            device_id=place, device_id_type=MESH)
        copy.wait_recv()
        copy.wait_send()
        return carry

    lax.fori_loop(1, peers, finish, 0)
    own.wait()


def exchange(which, gx_count, gy_count, e_right, e_left, lo, hi, mail):
    vm = pl.BlockSpec(memory_space=pltpu.VMEM)
    sem = pltpu.SemaphoreType.DMA
    f32 = jnp.float32
    peers = gx_count * gy_count
    return pl.pallas_call(
        functools.partial(exchange_kernel, gx_count, gy_count),
        out_shape=[
            jax.ShapeDtypeStruct(e_right.shape, f32),
            jax.ShapeDtypeStruct(e_left.shape, f32),
            jax.ShapeDtypeStruct((gx_count,) + lo.shape, f32),
            jax.ShapeDtypeStruct((gx_count,) + hi.shape, f32),
            jax.ShapeDtypeStruct(mail.shape, f32),
        ],
        in_specs=[vm] * 5,
        out_specs=[vm] * 5,
        scratch_shapes=[sem((2,)), sem((2,))] + [sem((gx_count,))] * 4 + [sem((peers,)), sem((peers,)), sem],
        compiler_params=pltpu.CompilerParams(
            collective_id=which, has_side_effects=True, vmem_limit_bytes=8 * MIB),
        name="exchange_%d" % which,
    )(e_right, e_left, lo, hi, mail)


def column(count):
    peers = count.shape[1]
    return jnp.broadcast_to(count.astype(jnp.float32), (8, peers)).T[:, 0:1].astype(jnp.int32)


def put_ends(new, i, dims, e_right, e_left, lo, hi):
    nz, cy, cx = dims
    at = pl.ds(pl.multiple_of(i * 128, 128), 128)
    lanes = lax.broadcasted_iota(jnp.int32, (128, 128), 1)
    ends = pltpu.roll(jnp.where(lanes < 64, new[:, :128], new[:, cx - 128:]), 2, 1).T
    e_right[:, at] = ends[0:2]
    e_left[:, at] = ends[2:4]
    for k in range(128 // cy):
        z = i * (128 // cy) + k
        for row in range(2):
            lo[row, pl.ds(z, 1)] = new[k * cy + row:k * cy + row + 1]
            hi[row, pl.ds(z, 1)] = new[k * cy + cy - 2 + row:k * cy + cy - 1 + row]


def prepare_kernel(dims, f, cell, temp, coef, heat, count, e_right, e_left, lo, hi, mail):
    nz, cy, cx = dims
    slot = lax.broadcasted_iota(jnp.int32, coef.shape[1:], 1)
    live = jnp.where(slot < column(count[...]), coef[0], 0.0)
    mail[:, 0, :] = jnp.concatenate([cell[0].astype(jnp.float32), temp[0]], axis=1)
    mail[:, 1, :] = jnp.concatenate([live, heat[0]], axis=1)

    def part(i, carry):
        put_ends(f[pl.ds(pl.multiple_of(i * 128, 128), 128)], i, dims, e_right, e_left, lo, hi)
        return carry

    lax.fori_loop(0, nz * cy // 128, part, 0)


def ends_shapes(dims):
    nz, cy, cx = dims
    return ([jax.ShapeDtypeStruct((2, nz * cy), jnp.float32)] * 2
            + [jax.ShapeDtypeStruct((2, nz, cx), jnp.float32)] * 2)


def prepare(dims, f, cell, temp, coef, heat, count):
    vm = pl.BlockSpec(memory_space=pltpu.VMEM)
    peers, cap = cell.shape[1:]
    return pl.pallas_call(
        functools.partial(prepare_kernel, dims),
        out_shape=ends_shapes(dims) + [jax.ShapeDtypeStruct((peers, 2, 2 * cap), jnp.float32)],
        in_specs=[vm] * 6,
        out_specs=[vm] * 5,
        compiler_params=pltpu.CompilerParams(vmem_limit_bytes=8 * MIB),
        name="prepare",
    )(f, cell, temp, coef, heat, count)


def stencil(dims, full_y, f, vel, o_left, o_right, y_up, y_low, info, xe, yg, ring, store):
    nz, cy, cx = dims
    gx_count = y_up.shape[0]
    k8 = lax.broadcasted_iota(jnp.int32, (8, 128), 0)
    l8 = lax.broadcasted_iota(jnp.int32, (8, 128), 1)
    hot = ((k8 == 0) & (l8 == 126)) | ((k8 == 1) & (l8 == 127)) | ((k8 == 2) & (l8 == 0)) | ((k8 == 3) & (l8 == 1))
    place = jnp.where(hot, 1.0, 0.0).astype(jnp.float32)
    edges = jnp.concatenate(
        [o_left[...], o_right[...], jnp.zeros((4, nz * cy), jnp.float32)], axis=0)
    xe[...] = lax.dot_general(
        edges, place, (((0,), (0,)), ((), ())), precision=lax.Precision.HIGHEST,
        preferred_element_type=jnp.float32)

    lane = lax.broadcasted_iota(jnp.int32, (nz, cx), 1)
    for src, q_at, base in ((y_up, 0, 0), (y_low, 2, 2)):
        q = info[q_at]
        rem = info[q_at + 1]
        nxt = lax.rem(q + 1, gx_count)
        turn = lax.rem(cx - rem, cx)
        for row in range(2):
            a = pltpu.roll(src[q, row], turn, 1)
            b = pltpu.roll(src[nxt, row], turn, 1)
            yg[base + row] = jnp.where(lane < cx - rem, a, b)

    start = (info[4] * cy).astype(jnp.float32)
    rows = lax.broadcasted_iota(jnp.int32, (cy, cx), 0).astype(jnp.float32) + start
    mean_flow = mean_speed * (2.0 * (rows + 0.5) * (1.0 / full_y) - 1.0)
    c8 = 8.0 / 12.0
    c1 = 1.0 / 12.0
    d16 = diffusivity * 16.0 / 12.0
    d1 = diffusivity / 12.0
    d30 = diffusivity * 90.0 / 12.0

    def plane(z, carry):
        c = f[pl.ds(pl.multiple_of(z * cy, cy), cy)]
        zm2 = f[pl.ds(pl.multiple_of(lax.rem(z + nz - 2, nz) * cy, cy), cy)]
        zm1 = f[pl.ds(pl.multiple_of(lax.rem(z + nz - 1, nz) * cy, cy), cy)]
        zp1 = f[pl.ds(pl.multiple_of(lax.rem(z + 1, nz) * cy, cy), cy)]
        zp2 = f[pl.ds(pl.multiple_of(lax.rem(z + 2, nz) * cy, cy), cy)]
        ring[0:cy] = c
        ring[cy:cy + 1] = yg[0, pl.ds(z, 1)]
        ring[cy + 1:cy + 2] = yg[1, pl.ds(z, 1)]
        ring[cy + 6:cy + 7] = yg[2, pl.ds(z, 1)]
        ring[cy + 7:cy + 8] = yg[3, pl.ds(z, 1)]
        ry = ring[...]
        ym2 = pltpu.roll(ry, 2, 0)[:cy]
        ym1 = pltpu.roll(ry, 1, 0)[:cy]
        yp1 = pltpu.roll(ry, cy + 7, 0)[:cy]
        yp2 = pltpu.roll(ry, cy + 6, 0)[:cy]
        rx = jnp.concatenate([c, xe[pl.ds(pl.multiple_of(z * cy, cy), cy)]], axis=1)
        wide = cx + 128
        xm2 = pltpu.roll(rx, 2, 1)[:, :cx]
        xm1 = pltpu.roll(rx, 1, 1)[:, :cx]
        xp1 = pltpu.roll(rx, wide - 1, 1)[:, :cx]
        xp2 = pltpu.roll(rx, wide - 2, 1)[:, :cx]
        u = vel[0, z].astype(jnp.float32) + mean_flow
        v = vel[1, z].astype(jnp.float32)
        w = vel[2, z].astype(jnp.float32)
        gx_ = c8 * (xp1 - xm1) - c1 * (xp2 - xm2)
        gy_ = c8 * (yp1 - ym1) - c1 * (yp2 - ym2)
        gz_ = c8 * (zp1 - zm1) - c1 * (zp2 - zm2)
        near = ((xp1 + xm1) + (yp1 + ym1)) + (zp1 + zm1)
        far = ((xp2 + xm2) + (yp2 + ym2)) + (zp2 + zm2)
        rhs = (d16 * near - d1 * far - d30 * c) - u * gx_ - v * (gy_ + mean_gradient) - w * gz_
        euler = c + time_step * rhs
        store(z, pl.ds(pl.multiple_of(z * cy, cy), cy), euler)
        return carry

    lax.fori_loop(0, nz, plane, 0, unroll=2)


def particles(second, rows, rt, now, nxt, field, accs, buf, peers):
    cx = field.shape[1]
    cap = buf.shape[1]
    scale = time_step * heat_share * (0.25 if second else 1.0)
    lane = lax.broadcasted_iota(jnp.int32, (cap, cx), 1)
    src = lax.broadcasted_iota(jnp.int32, (cap, LANES), 1)

    def group(b, carry):
        s = b * GROUP
        turn = lax.rem(LANES - s, LANES)
        t = pltpu.roll(rt[...], turn, 1)
        old = pltpu.roll(now[...], turn, 1)
        made = nxt[...]
        for g in range(GROUP):
            for i in range(cap):
                buf[g, i:i + 1] = field[pl.ds(rows[s + g, i], 1)]
        for g in range(GROUP):
            hit = lane == t[0:cap, g:g + 1].astype(jnp.int32) % cx
            sample = jnp.sum(jnp.where(hit, buf[g], 0.0), axis=1, keepdims=True)
            temp = old[:, g:g + 1]
            flux = t[2 * cap:3 * cap, g:g + 1] * (temp - sample)
            new = temp + time_step * (t[3 * cap:, g:g + 1] - flux)
            if second:
                new = 0.75 * t[cap:2 * cap, g:g + 1] + 0.25 * new
            made = jnp.where(src == s + g, new, made)
            buf[g] = jnp.where(hit, scale * flux, 0.0)
        nxt[...] = made
        for g in range(GROUP):
            for i in range(0, cap, WAYS):
                ats = [pl.ds(rows[s + g, i + k], 1) for k in range(WAYS)]
                adds = [accs[k][ats[k]] + buf[g, i + k:i + k + 1] for k in range(WAYS)]
                for k in range(WAYS):
                    accs[k][ats[k]] = adds[k]
        return carry

    lax.fori_loop(0, peers // GROUP, group, 0)


def first_kernel(dims, full_y, f, vel, o_left, o_right, y_up, y_low, came, info, rows,
                 s1, q2, e_right, e_left, lo, hi, home,
                 xe, yg, ring, rt, t1, t2, buf, acc1, acc2, acc3):
    nz, cy, cx = dims
    peers = came.shape[0]
    cap = home.shape[2]
    zero = jnp.zeros((cy, cx), jnp.float32)

    def store(z, at, euler):
        s1[at] = euler
        for acc in (q2, acc1, acc2, acc3):
            acc[at] = zero

    stencil(dims, full_y, f, vel, o_left, o_right, y_up, y_low, info, xe, yg, ring, store)
    for half in range(2):
        got = came[:, half, :]
        if peers < LANES:
            got = jnp.concatenate([got, jnp.zeros((LANES - peers, 2 * cap), jnp.float32)], axis=0)
        rt[2 * cap * half:2 * cap * (half + 1)] = got.T
    t1[...] = jnp.zeros_like(t1)
    t2[...] = jnp.zeros_like(t2)
    particles(False, rows, rt, rt.at[cap:2 * cap], t1, f, (s1, acc1, acc2, acc3), buf, peers)

    def total_one(i, carry):
        at = pl.ds(pl.multiple_of(i * 128, 128), 128)
        new = (s1[at] + acc1[at]) + (acc2[at] + acc3[at])
        s1[at] = new
        for acc in (acc1, acc2, acc3):
            acc[at] = jnp.zeros_like(new)
        put_ends(new, i, dims, e_right, e_left, lo, hi)
        return carry

    lax.fori_loop(0, nz * cy // 128, total_one, 0)
    particles(True, rows, rt, t1, t2, s1, (q2, acc1, acc2, acc3), buf, peers)
    home[:, 0, :] = t2[...].T[:peers]

    def total_two(i, carry):
        at = pl.ds(pl.multiple_of(i * 64, 64), 64)
        q2[at] = (q2[at] + acc1[at]) + (acc2[at] + acc3[at])
        return carry

    lax.fori_loop(0, nz * cy // 64, total_two, 0)


def work_space(dims):
    nz, cy, cx = dims
    f32 = jnp.float32
    return [pltpu.VMEM((nz * cy, 128), f32), pltpu.VMEM((4, nz, cx), f32), pltpu.VMEM((cy + 8, cx), f32)]


def first(dims, full_y, cap, f, vel, halos, came, info, rows):
    nz, cy, cx = dims
    f32 = jnp.float32
    vm = pl.BlockSpec(memory_space=pltpu.VMEM)
    sm = pl.BlockSpec(memory_space=pltpu.SMEM)
    grid = jax.ShapeDtypeStruct((nz * cy, cx), f32)
    space = pltpu.VMEM((nz * cy, cx), f32)
    return pl.pallas_call(
        functools.partial(first_kernel, dims, full_y),
        out_shape=[grid, grid] + ends_shapes(dims) + [jax.ShapeDtypeStruct((came.shape[0], 1, cap), f32)],
        in_specs=[vm] * 7 + [sm, sm],
        out_specs=[vm] * 7,
        scratch_shapes=work_space(dims) + [
            pltpu.VMEM((4 * cap, LANES), f32), pltpu.VMEM((cap, LANES), f32), pltpu.VMEM((cap, LANES), f32),
            pltpu.VMEM((GROUP, cap, cx), f32), space, space, space],
        compiler_params=pltpu.CompilerParams(vmem_limit_bytes=26 * MIB),
        name="section_one",
    )(f, vel, *halos, came, info, rows)


def second_kernel(dims, full_y, f, vel, o_left, o_right, y_up, y_low, f0, q2, home, count, info,
                  out, temp_out, xe, yg, ring):
    def store(z, at, euler):
        out[z] = 0.75 * f0[at] + 0.25 * euler + q2[at]

    back = home[:, 0, :]
    slot = lax.broadcasted_iota(jnp.int32, back.shape, 1)
    temp_out[0] = jnp.where(slot < column(count[...]), back, 0.0)
    stencil(dims, full_y, f, vel, o_left, o_right, y_up, y_low, info, xe, yg, ring, store)


def second(dims, full_y, f, vel, halos, f0, q2, home, count, info):
    f32 = jnp.float32
    vm = pl.BlockSpec(memory_space=pltpu.VMEM)
    return pl.pallas_call(
        functools.partial(second_kernel, dims, full_y),
        out_shape=[jax.ShapeDtypeStruct(dims, f32),
                   jax.ShapeDtypeStruct((1, home.shape[0], home.shape[2]), f32)],
        in_specs=[vm] * 10 + [pl.BlockSpec(memory_space=pltpu.SMEM)],
        out_specs=[vm] * 2,
        scratch_shapes=work_space(dims),
        compiler_params=pltpu.CompilerParams(vmem_limit_bytes=26 * MIB),
        name="section_two",
    )(f, vel, *halos, f0, q2, home, count, info)


def on_device(
    scalar_field, velocity, shear_offset, part_temp, part_coef, part_heat, part_cell, part_count
):
    nz, cy, cx = scalar_field.shape
    cap = part_temp.shape[2]
    gx_index = lax.axis_index("gx")
    gy_index = lax.axis_index("gy")
    gx_count = lax.axis_size("gx")
    gy_count = lax.axis_size("gy")
    full_x = cx * gx_count
    full_y = cy * gy_count
    dims = (nz, cy, cx)
    field = scalar_field.reshape(nz * cy, cx)

    def info(offset):
        low_shift = jnp.where(gy_index == 0, (full_x - offset) % full_x, 0)
        high_shift = jnp.where(gy_index == gy_count - 1, offset, 0)
        up = (gx_index * cx - high_shift) % full_x
        low = (gx_index * cx - low_shift) % full_x
        return jnp.stack([up // cx, up % cx, low // cx, low % cx, gy_index]).astype(jnp.int32)

    sends = prepare(dims, field, part_cell, part_temp, part_coef, part_heat, part_count)
    *halos, came = exchange(0, gx_count, gy_count, *sends)
    rows = came[:, 0, :cap].astype(jnp.int32) // cx
    section_one, source, *sends = first(
        dims, full_y, cap, field, velocity, halos, came, info(shear_offset[0]), rows)
    *halos, home = exchange(1, gx_count, gy_count, *sends)
    scalar_out, temp_out = second(
        dims, full_y, section_one, velocity, halos, field, source, home, part_count,
        info(shear_offset[1]))
    return (scalar_out, temp_out)


def solution(mesh):
    in_specs = (
        P(None, "gy", "gx"),
        P(None, None, "gy", "gx"),
        P(),
        P(("gx", "gy"), None, None),
        P(("gx", "gy"), None, None),
        P(("gx", "gy"), None, None),
        P(("gx", "gy"), None, None),
        P(("gx", "gy"), None),
    )
    out_specs = (P(None, "gy", "gx"), P(("gx", "gy"), None, None))
    return jax.shard_map(
        on_device, mesh=mesh, in_specs=in_specs, out_specs=out_specs, check_vma=False
    )
```

```python
import functools

import jax
import jax.numpy as jnp
from jax import lax
from jax.experimental import pallas as pl
from jax.experimental.pallas import tpu as pltpu
from jax.sharding import PartitionSpec as P

time_step = 0.1
diffusivity = 0.1
mean_speed = 1.0
mean_gradient = 1.0
heat_share = 0.5

MESH = pl.DeviceIdType.MESH
MIB = 1 << 20
GROUP = 8
LANES = 128
WAYS = 4


def exchange_kernel(gx_count, gy_count, loads, *refs):
    if loads:
        e_right, e_left, lo, hi, mail, held, o_left, o_right, y_up, y_low, came, near = refs[:12]
        send_x, recv_x, send_lo, recv_up, send_hi, recv_low, send_p, recv_p, own_sem, load_sem = refs[12:]
        vel = (held, near, load_sem)
    else:
        e_right, e_left, lo, hi, mail, o_left, o_right, y_up, y_low, came = refs[:10]
        send_x, recv_x, send_lo, recv_up, send_hi, recv_low, send_p, recv_p, own_sem = refs[10:]
        vel = None
    gx = lax.axis_index("gx")
    gy = lax.axis_index("gy")
    right = lax.rem(gx + 1, gx_count)
    left = lax.rem(gx + gx_count - 1, gx_count)
    first = gy == 0
    last = gy == gy_count - 1

    barrier = pltpu.get_barrier_semaphore()

    me = gx * gy_count + gy
    xs = [gx] + [lax.rem(gx + i, gx_count) for i in range(1, gx_count)]
    ys = [gy] + [lax.rem(gy + i, gy_count) for i in range(1, gy_count)]
    others = [(x * gy_count + y, (x, y)) for y in ys for x in xs][1:]
    for _, place in others:
        pl.semaphore_signal(barrier, inc=1, device_id=place, device_id_type=MESH)
    own = pltpu.make_async_copy(mail.at[me], came.at[me], own_sem)
    own.start()
    load = None
    if vel is not None:
        load = pltpu.make_async_copy(vel[0], vel[1], vel[2])
        load.start()
    pl.semaphore_wait(barrier, len(others))

    def copy_x(src, dst, k, x):
        return pltpu.make_async_remote_copy(
            src_ref=src, dst_ref=dst, send_sem=send_x.at[k], recv_sem=recv_x.at[k],
            device_id=(x, gy), device_id_type=MESH)

    def copy_lo(g, x, y):
        return pltpu.make_async_remote_copy(
            src_ref=lo, dst_ref=y_up.at[gx], send_sem=send_lo.at[g], recv_sem=recv_up.at[gx],
            device_id=(x, y), device_id_type=MESH)

    def copy_hi(g, x, y):
        return pltpu.make_async_remote_copy(
            src_ref=hi, dst_ref=y_low.at[gx], send_sem=send_hi.at[g], recv_sem=recv_low.at[gx],
            device_id=(x, y), device_id_type=MESH)

    def all_copies(act):
        @pl.when(first)
        def _():
            for g in range(gx_count):
                act(copy_lo(g, g, gy_count - 1))

        @pl.when(last)
        def _():
            for g in range(gx_count):
                act(copy_hi(g, g, 0))

        @pl.when(jnp.logical_not(first))
        def _():
            act(copy_lo(0, gx, gy - 1))

        @pl.when(jnp.logical_not(last))
        def _():
            act(copy_hi(0, gx, gy + 1))

    all_copies(lambda c: c.start())
    to_right = copy_x(e_right, o_left, 0, right)
    to_left = copy_x(e_left, o_right, 1, left)
    to_right.start()
    to_left.start()

    for d, place in others:
        pltpu.make_async_remote_copy(
            src_ref=mail.at[d], dst_ref=came.at[me], send_sem=send_p.at[d], recv_sem=recv_p.at[me],
            device_id=place, device_id_type=MESH).start()

    def arrive(rows, slots, sems, s):
        pltpu.make_async_remote_copy(
            src_ref=rows, dst_ref=slots.at[s], send_sem=send_lo.at[0], recv_sem=sems.at[s],
            device_id=(right, gy), device_id_type=MESH).wait_recv()

    @pl.when(last)
    def _():
        for s in range(gx_count):
            arrive(lo, y_up, recv_up, s)

    @pl.when(jnp.logical_not(last))
    def _():
        arrive(lo, y_up, recv_up, gx)

    @pl.when(first)
    def _():
        for s in range(gx_count):
            arrive(hi, y_low, recv_low, s)

    @pl.when(jnp.logical_not(first))
    def _():
        arrive(hi, y_low, recv_low, gx)

    to_right.wait_recv()
    to_left.wait_recv()
    all_copies(lambda c: c.wait_send())
    to_right.wait_send()
    to_left.wait_send()

    for d, place in others:
        copy = pltpu.make_async_remote_copy(
            src_ref=mail.at[d], dst_ref=came.at[d], send_sem=send_p.at[d], recv_sem=recv_p.at[d],
            device_id=place, device_id_type=MESH)
        copy.wait_recv()
        copy.wait_send()
    own.wait()
    if load is not None:
        load.wait()


def exchange(which, gx_count, gy_count, e_right, e_left, lo, hi, mail, *held):
    vm = pl.BlockSpec(memory_space=pltpu.VMEM)
    sem = pltpu.SemaphoreType.DMA
    f32 = jnp.float32
    peers = gx_count * gy_count
    return pl.pallas_call(
        functools.partial(exchange_kernel, gx_count, gy_count, bool(held)),
        out_shape=[
            jax.ShapeDtypeStruct(e_right.shape, f32),
            jax.ShapeDtypeStruct(e_left.shape, f32),
            jax.ShapeDtypeStruct((gx_count,) + lo.shape, f32),
            jax.ShapeDtypeStruct((gx_count,) + hi.shape, f32),
            jax.ShapeDtypeStruct(mail.shape, f32),
        ] + [jax.ShapeDtypeStruct(h.shape, h.dtype) for h in held],
        in_specs=[vm] * 5 + [pl.BlockSpec(memory_space=pltpu.HBM)] * len(held),
        out_specs=[vm] * (5 + len(held)),
        scratch_shapes=[sem((2,)), sem((2,))] + [sem((gx_count,))] * 4 + [sem((peers,)), sem((peers,)), sem] + [sem] * len(held),
        compiler_params=pltpu.CompilerParams(
            collective_id=which, has_side_effects=True, vmem_limit_bytes=8 * MIB),
        name="exchange_%d" % which,
    )(e_right, e_left, lo, hi, mail, *held)


def column(count):
    peers = count.shape[1]
    return jnp.broadcast_to(count.astype(jnp.float32), (8, peers)).T[:, 0:1].astype(jnp.int32)


def put_ends(new, i, dims, e_right, e_left, lo, hi):
    nz, cy, cx = dims
    at = pl.ds(pl.multiple_of(i * 128, 128), 128)
    lanes = lax.broadcasted_iota(jnp.int32, (128, 128), 1)
    ends = pltpu.roll(jnp.where(lanes < 64, new[:, :128], new[:, cx - 128:]), 2, 1).T
    e_right[:, at] = ends[0:2]
    e_left[:, at] = ends[2:4]
    for k in range(128 // cy):
        z = i * (128 // cy) + k
        for row in range(2):
            lo[row, pl.ds(z, 1)] = new[k * cy + row:k * cy + row + 1]
            hi[row, pl.ds(z, 1)] = new[k * cy + cy - 2 + row:k * cy + cy - 1 + row]


def prepare_kernel(dims, f_at, cell_at, temp_at, coef_at, heat_at, count_at,
                   e_right, e_left, lo, hi, mail, f, cell, temp, coef, heat, count, sems):
    nz, cy, cx = dims
    pairs = ((cell_at, cell), (temp_at, temp), (coef_at, coef), (heat_at, heat), (count_at, count), (f_at, f))
    copies = [pltpu.make_async_copy(a, b, sems.at[k]) for k, (a, b) in enumerate(pairs)]
    for c in copies:
        c.start()
    for c in copies[:-1]:
        c.wait()
    slot = lax.broadcasted_iota(jnp.int32, coef.shape[1:], 1)
    live = jnp.where(slot < column(count[...]), coef[0], 0.0)
    mail[:, 0, :] = jnp.concatenate([cell[0].astype(jnp.float32), temp[0]], axis=1)
    mail[:, 1, :] = jnp.concatenate([live, heat[0]], axis=1)

    copies[-1].wait()

    def part(i, carry):
        put_ends(f[pl.ds(pl.multiple_of(i * 128, 128), 128)], i, dims, e_right, e_left, lo, hi)
        return carry

    lax.fori_loop(0, nz * cy // 128, part, 0)


def ends_shapes(dims):
    nz, cy, cx = dims
    return ([jax.ShapeDtypeStruct((2, nz * cy), jnp.float32)] * 2
            + [jax.ShapeDtypeStruct((2, nz, cx), jnp.float32)] * 2)


def prepare(dims, f, cell, temp, coef, heat, count):
    vm = pl.BlockSpec(memory_space=pltpu.VMEM)
    peers, cap = cell.shape[1:]
    return pl.pallas_call(
        functools.partial(prepare_kernel, dims),
        out_shape=ends_shapes(dims) + [
            jax.ShapeDtypeStruct((peers, 2, 2 * cap), jnp.float32),
            jax.ShapeDtypeStruct(f.shape, f.dtype)],
        in_specs=[pl.BlockSpec(memory_space=pltpu.HBM)] * 6,
        out_specs=[vm] * 6,
        scratch_shapes=[pltpu.VMEM(a.shape, a.dtype) for a in (cell, temp, coef, heat, count)]
        + [pltpu.SemaphoreType.DMA((6,))],
        compiler_params=pltpu.CompilerParams(vmem_limit_bytes=8 * MIB),
        name="prepare",
    )(f, cell, temp, coef, heat, count)


def plan(which, dims, shear, gx_count, gy_count):
    cx = dims[2]
    gx = lax.axis_index("gx")
    gy = lax.axis_index("gy")
    full_x = cx * gx_count
    offset = shear[which]
    up = lax.rem(gx * cx + full_x - jnp.where(gy == gy_count - 1, offset, 0), full_x)
    low = lax.rem(gx * cx + jnp.where(gy == 0, offset, 0), full_x)
    return lax.div(up, cx), lax.rem(up, cx), lax.div(low, cx), lax.rem(low, cx), gy


def stencil(dims, full_y, f, vel, o_left, o_right, y_up, y_low, info, xe, yg, ring, store):
    nz, cy, cx = dims
    gx_count = y_up.shape[0]
    k8 = lax.broadcasted_iota(jnp.int32, (8, 128), 0)
    l8 = lax.broadcasted_iota(jnp.int32, (8, 128), 1)
    hot = ((k8 == 0) & (l8 == 126)) | ((k8 == 1) & (l8 == 127)) | ((k8 == 2) & (l8 == 0)) | ((k8 == 3) & (l8 == 1))
    place = jnp.where(hot, 1.0, 0.0).astype(jnp.float32)
    edges = jnp.concatenate(
        [o_left[...], o_right[...], jnp.zeros((4, nz * cy), jnp.float32)], axis=0)
    xe[...] = lax.dot_general(
        edges, place, (((0,), (0,)), ((), ())), precision=lax.Precision.HIGHEST,
        preferred_element_type=jnp.float32)

    lane = lax.broadcasted_iota(jnp.int32, (nz, cx), 1)
    for src, q_at, base in ((y_up, 0, 0), (y_low, 2, 2)):
        q = info[q_at]
        rem = info[q_at + 1]
        nxt = lax.rem(q + 1, gx_count)
        turn = lax.rem(cx - rem, cx)
        for row in range(2):
            a = pltpu.roll(src[q, row], turn, 1)
            b = pltpu.roll(src[nxt, row], turn, 1)
            yg[base + row] = jnp.where(lane < cx - rem, a, b)

    start = (info[4] * cy).astype(jnp.float32)
    rows = lax.broadcasted_iota(jnp.int32, (cy, cx), 0).astype(jnp.float32) + start
    mean_flow = mean_speed * (2.0 * (rows + 0.5) * (1.0 / full_y) - 1.0)
    c8 = 8.0 / 12.0
    c1 = 1.0 / 12.0
    d16 = diffusivity * 16.0 / 12.0
    d1 = diffusivity / 12.0
    d30 = diffusivity * 90.0 / 12.0

    def plane(z, carry):
        c = f[pl.ds(pl.multiple_of(z * cy, cy), cy)]
        zm2 = f[pl.ds(pl.multiple_of(lax.rem(z + nz - 2, nz) * cy, cy), cy)]
        zm1 = f[pl.ds(pl.multiple_of(lax.rem(z + nz - 1, nz) * cy, cy), cy)]
        zp1 = f[pl.ds(pl.multiple_of(lax.rem(z + 1, nz) * cy, cy), cy)]
        zp2 = f[pl.ds(pl.multiple_of(lax.rem(z + 2, nz) * cy, cy), cy)]
        ring[0:cy] = c
        ring[cy:cy + 1] = yg[0, pl.ds(z, 1)]
        ring[cy + 1:cy + 2] = yg[1, pl.ds(z, 1)]
        ring[cy + 6:cy + 7] = yg[2, pl.ds(z, 1)]
        ring[cy + 7:cy + 8] = yg[3, pl.ds(z, 1)]
        ry = ring[...]
        ym2 = pltpu.roll(ry, 2, 0)[:cy]
        ym1 = pltpu.roll(ry, 1, 0)[:cy]
        yp1 = pltpu.roll(ry, cy + 7, 0)[:cy]
        yp2 = pltpu.roll(ry, cy + 6, 0)[:cy]
        rx = jnp.concatenate([c, xe[pl.ds(pl.multiple_of(z * cy, cy), cy)]], axis=1)
        wide = cx + 128
        xm2 = pltpu.roll(rx, 2, 1)[:, :cx]
        xm1 = pltpu.roll(rx, 1, 1)[:, :cx]
        xp1 = pltpu.roll(rx, wide - 1, 1)[:, :cx]
        xp2 = pltpu.roll(rx, wide - 2, 1)[:, :cx]
        u = vel[0, z].astype(jnp.float32) + mean_flow
        v = vel[1, z].astype(jnp.float32)
        w = vel[2, z].astype(jnp.float32)
        gx_ = c8 * (xp1 - xm1) - c1 * (xp2 - xm2)
        gy_ = c8 * (yp1 - ym1) - c1 * (yp2 - ym2)
        gz_ = c8 * (zp1 - zm1) - c1 * (zp2 - zm2)
        near = ((xp1 + xm1) + (yp1 + ym1)) + (zp1 + zm1)
        far = ((xp2 + xm2) + (yp2 + ym2)) + (zp2 + zm2)
        rhs = (d16 * near - d1 * far - d30 * c) - u * gx_ - v * (gy_ + mean_gradient) - w * gz_
        euler = c + time_step * rhs
        store(z, pl.ds(pl.multiple_of(z * cy, cy), cy), euler)
        return carry

    lax.fori_loop(0, nz, plane, 0, unroll=2)


def particles(second, rows, rt, now, nxt, field, accs, buf, peers):
    cx = field.shape[1]
    cap = buf.shape[1]
    scale = time_step * heat_share * (0.25 if second else 1.0)
    lane = lax.broadcasted_iota(jnp.int32, (cap, cx), 1)
    src = lax.broadcasted_iota(jnp.int32, (cap, LANES), 1)

    def group(b, carry):
        s = b * GROUP
        turn = lax.rem(LANES - s, LANES)
        t = pltpu.roll(rt[...], turn, 1)
        old = pltpu.roll(now[...], turn, 1)
        made = nxt[...]
        for g in range(GROUP):
            for i in range(cap):
                buf[g, i:i + 1] = field[pl.ds(rows[s + g, i], 1)]
        for g in range(GROUP):
            hit = lane == t[0:cap, g:g + 1].astype(jnp.int32) % cx
            sample = jnp.sum(jnp.where(hit, buf[g], 0.0), axis=1, keepdims=True)
            temp = old[:, g:g + 1]
            flux = t[2 * cap:3 * cap, g:g + 1] * (temp - sample)
            new = temp + time_step * (t[3 * cap:, g:g + 1] - flux)
            if second:
                new = 0.75 * t[cap:2 * cap, g:g + 1] + 0.25 * new
            made = jnp.where(src == s + g, new, made)
            buf[g] = jnp.where(hit, scale * flux, 0.0)
        nxt[...] = made
        for g in range(GROUP):
            for i in range(0, cap, WAYS):
                ats = [pl.ds(rows[s + g, i + k], 1) for k in range(WAYS)]
                adds = [accs[k][ats[k]] + buf[g, i + k:i + k + 1] for k in range(WAYS)]
                for k in range(WAYS):
                    accs[k][ats[k]] = adds[k]
        return carry

    lax.fori_loop(0, peers // GROUP, group, 0)


def first_kernel(dims, full_y, f, vel, o_left, o_right, y_up, y_low, came, shear, rows,
                 s1, q2, e_right, e_left, lo, hi, home,
                 xe, yg, ring, rt, t1, t2, buf, acc1, acc2, acc3):
    nz, cy, cx = dims
    peers = came.shape[0]
    cap = home.shape[2]
    zero = jnp.zeros((cy, cx), jnp.float32)
    info = plan(0, dims, shear, y_up.shape[0], full_y // cy)

    def store(z, at, euler):
        s1[at] = euler
        for acc in (q2, acc1, acc2, acc3):
            acc[at] = zero

    stencil(dims, full_y, f, vel, o_left, o_right, y_up, y_low, info, xe, yg, ring, store)
    for half in range(2):
        got = came[:, half, :]
        if peers < LANES:
            got = jnp.concatenate([got, jnp.zeros((LANES - peers, 2 * cap), jnp.float32)], axis=0)
        rt[2 * cap * half:2 * cap * (half + 1)] = got.T
    t1[...] = jnp.zeros_like(t1)
    t2[...] = jnp.zeros_like(t2)
    particles(False, rows, rt, rt.at[cap:2 * cap], t1, f, (s1, acc1, acc2, acc3), buf, peers)

    def total_one(i, carry):
        at = pl.ds(pl.multiple_of(i * 128, 128), 128)
        new = (s1[at] + acc1[at]) + (acc2[at] + acc3[at])
        s1[at] = new
        for acc in (acc1, acc2, acc3):
            acc[at] = jnp.zeros_like(new)
        put_ends(new, i, dims, e_right, e_left, lo, hi)
        return carry

    lax.fori_loop(0, nz * cy // 128, total_one, 0)
    particles(True, rows, rt, t1, t2, s1, (q2, acc1, acc2, acc3), buf, peers)
    home[:, 0, :] = t2[...].T[:peers]

    def total_two(i, carry):
        at = pl.ds(pl.multiple_of(i * 64, 64), 64)
        q2[at] = (q2[at] + acc1[at]) + (acc2[at] + acc3[at])
        return carry

    lax.fori_loop(0, nz * cy // 64, total_two, 0)


def work_space(dims):
    nz, cy, cx = dims
    f32 = jnp.float32
    return [pltpu.VMEM((nz * cy, 128), f32), pltpu.VMEM((4, nz, cx), f32), pltpu.VMEM((cy + 8, cx), f32)]


def first(dims, full_y, cap, f, vel, halos, came, info, rows):
    nz, cy, cx = dims
    f32 = jnp.float32
    vm = pl.BlockSpec(memory_space=pltpu.VMEM)
    sm = pl.BlockSpec(memory_space=pltpu.SMEM)
    grid = jax.ShapeDtypeStruct((nz * cy, cx), f32)
    space = pltpu.VMEM((nz * cy, cx), f32)
    return pl.pallas_call(
        functools.partial(first_kernel, dims, full_y),
        out_shape=[grid, grid] + ends_shapes(dims) + [jax.ShapeDtypeStruct((came.shape[0], 1, cap), f32)],
        in_specs=[vm] * 7 + [sm, sm],
        out_specs=[vm] * 7,
        scratch_shapes=work_space(dims) + [
            pltpu.VMEM((4 * cap, LANES), f32), pltpu.VMEM((cap, LANES), f32), pltpu.VMEM((cap, LANES), f32),
            pltpu.VMEM((GROUP, cap, cx), f32), space, space, space],
        compiler_params=pltpu.CompilerParams(vmem_limit_bytes=26 * MIB),
        name="section_one",
    )(f, vel, *halos, came, info, rows)


def second_kernel(dims, full_y, f, vel, o_left, o_right, y_up, y_low, f0, q2, home, count, shear,
                  out, temp_out, xe, yg, ring):
    info = plan(1, dims, shear, y_up.shape[0], full_y // dims[1])

    def store(z, at, euler):
        out[z] = 0.75 * f0[at] + 0.25 * euler + q2[at]

    back = home[:, 0, :]
    slot = lax.broadcasted_iota(jnp.int32, back.shape, 1)
    temp_out[0] = jnp.where(slot < column(count[...]), back, 0.0)
    stencil(dims, full_y, f, vel, o_left, o_right, y_up, y_low, info, xe, yg, ring, store)


def second(dims, full_y, f, vel, halos, f0, q2, home, count, info):
    f32 = jnp.float32
    vm = pl.BlockSpec(memory_space=pltpu.VMEM)
    return pl.pallas_call(
        functools.partial(second_kernel, dims, full_y),
        out_shape=[jax.ShapeDtypeStruct(dims, f32),
                   jax.ShapeDtypeStruct((1, home.shape[0], home.shape[2]), f32)],
        in_specs=[vm] * 10 + [pl.BlockSpec(memory_space=pltpu.SMEM)],
        out_specs=[vm] * 2,
        scratch_shapes=work_space(dims),
        compiler_params=pltpu.CompilerParams(vmem_limit_bytes=26 * MIB),
        name="section_two",
    )(f, vel, *halos, f0, q2, home, count, info)


def on_device(
    scalar_field, velocity, shear_offset, part_temp, part_coef, part_heat, part_cell, part_count
):
    nz, cy, cx = scalar_field.shape
    cap = part_temp.shape[2]
    gx_count = lax.axis_size("gx")
    gy_count = lax.axis_size("gy")
    full_y = cy * gy_count
    dims = (nz, cy, cx)
    field = scalar_field.reshape(nz * cy, cx)

    *sends, near_field = prepare(dims, field, part_cell, part_temp, part_coef, part_heat, part_count)
    *halos, came, near = exchange(0, gx_count, gy_count, *sends, velocity)
    rows = came[:, 0, :cap].astype(jnp.int32) // cx
    section_one, source, *sends = first(
        dims, full_y, cap, near_field, near, halos, came, shear_offset, rows)
    *halos, home = exchange(1, gx_count, gy_count, *sends)
    scalar_out, temp_out = second(
        dims, full_y, section_one, near, halos, near_field, source, home, part_count,
        shear_offset)
    return (scalar_out, temp_out)


def solution(mesh):
    in_specs = (
        P(None, "gy", "gx"),
        P(None, None, "gy", "gx"),
        P(),
        P(("gx", "gy"), None, None),
        P(("gx", "gy"), None, None),
        P(("gx", "gy"), None, None),
        P(("gx", "gy"), None, None),
        P(("gx", "gy"), None),
    )
    out_specs = (P(None, "gy", "gx"), P(("gx", "gy"), None, None))
    return jax.shard_map(
        on_device, mesh=mesh, in_specs=in_specs, out_specs=out_specs, check_vma=False
    )
```

```python
import functools

import jax
import jax.numpy as jnp
from jax import lax
from jax.experimental import pallas as pl
from jax.experimental.pallas import tpu as pltpu
from jax.sharding import PartitionSpec as P

time_step = 0.1
diffusivity = 0.1
mean_speed = 1.0
mean_gradient = 1.0
heat_share = 0.5

MESH = pl.DeviceIdType.MESH
MIB = 1 << 20
GROUP = 8
LANES = 128
WAYS = 4


def exchange_kernel(gx_count, gy_count, loads, *refs):
    if loads:
        e_right, e_left, lo, hi, mail, held, o_left, o_right, y_up, y_low, came, near = refs[:12]
        send_x, recv_x, send_lo, recv_up, send_hi, recv_low, send_p, recv_p, own_sem, load_sem = refs[12:]
        vel = (held, near, load_sem)
    else:
        e_right, e_left, lo, hi, mail, o_left, o_right, y_up, y_low, came = refs[:10]
        send_x, recv_x, send_lo, recv_up, send_hi, recv_low, send_p, recv_p, own_sem = refs[10:]
        vel = None
    gx = lax.axis_index("gx")
    gy = lax.axis_index("gy")
    right = lax.rem(gx + 1, gx_count)
    left = lax.rem(gx + gx_count - 1, gx_count)
    first = gy == 0
    last = gy == gy_count - 1

    barrier = pltpu.get_barrier_semaphore()

    me = gx * gy_count + gy
    xs = [gx] + [lax.rem(gx + i, gx_count) for i in range(1, gx_count)]
    ys = [gy] + [lax.rem(gy + i, gy_count) for i in range(1, gy_count)]
    others = [(x * gy_count + y, (x, y)) for y in ys for x in xs][1:]
    for _, place in others:
        pl.semaphore_signal(barrier, inc=1, device_id=place, device_id_type=MESH)
    own = pltpu.make_async_copy(mail.at[me], came.at[me], own_sem)
    own.start()
    load = None
    if vel is not None:
        load = pltpu.make_async_copy(vel[0], vel[1], vel[2])
        load.start()
    pl.semaphore_wait(barrier, len(others))

    def copy_x(src, dst, k, x):
        return pltpu.make_async_remote_copy(
            src_ref=src, dst_ref=dst, send_sem=send_x.at[k], recv_sem=recv_x.at[k],
            device_id=(x, gy), device_id_type=MESH)

    def copy_lo(g, x, y):
        return pltpu.make_async_remote_copy(
            src_ref=lo, dst_ref=y_up.at[gx], send_sem=send_lo.at[g], recv_sem=recv_up.at[gx],
            device_id=(x, y), device_id_type=MESH)

    def copy_hi(g, x, y):
        return pltpu.make_async_remote_copy(
            src_ref=hi, dst_ref=y_low.at[gx], send_sem=send_hi.at[g], recv_sem=recv_low.at[gx],
            device_id=(x, y), device_id_type=MESH)

    def all_copies(act):
        @pl.when(first)
        def _():
            for g in range(gx_count):
                act(copy_lo(g, g, gy_count - 1))

        @pl.when(last)
        def _():
            for g in range(gx_count):
                act(copy_hi(g, g, 0))

        @pl.when(jnp.logical_not(first))
        def _():
            act(copy_lo(0, gx, gy - 1))

        @pl.when(jnp.logical_not(last))
        def _():
            act(copy_hi(0, gx, gy + 1))

    to_right = copy_x(e_right, o_left, 0, right)
    to_left = copy_x(e_left, o_right, 1, left)
    to_right.start()
    to_left.start()

    for d, place in others:
        pltpu.make_async_remote_copy(
            src_ref=mail.at[d], dst_ref=came.at[me], send_sem=send_p.at[d], recv_sem=recv_p.at[me],
            device_id=place, device_id_type=MESH).start()
    all_copies(lambda c: c.start())

    def arrive(rows, slots, sems, s):
        pltpu.make_async_remote_copy(
            src_ref=rows, dst_ref=slots.at[s], send_sem=send_lo.at[0], recv_sem=sems.at[s],
            device_id=(right, gy), device_id_type=MESH).wait_recv()

    @pl.when(last)
    def _():
        for s in range(gx_count):
            arrive(lo, y_up, recv_up, s)

    @pl.when(jnp.logical_not(last))
    def _():
        arrive(lo, y_up, recv_up, gx)

    @pl.when(first)
    def _():
        for s in range(gx_count):
            arrive(hi, y_low, recv_low, s)

    @pl.when(jnp.logical_not(first))
    def _():
        arrive(hi, y_low, recv_low, gx)

    to_right.wait_recv()
    to_left.wait_recv()
    all_copies(lambda c: c.wait_send())
    to_right.wait_send()
    to_left.wait_send()

    for d, place in others:
        copy = pltpu.make_async_remote_copy(
            src_ref=mail.at[d], dst_ref=came.at[d], send_sem=send_p.at[d], recv_sem=recv_p.at[d],
            device_id=place, device_id_type=MESH)
        copy.wait_recv()
        copy.wait_send()
    own.wait()
    if load is not None:
        load.wait()


def exchange(which, gx_count, gy_count, e_right, e_left, lo, hi, mail, *held):
    vm = pl.BlockSpec(memory_space=pltpu.VMEM)
    sem = pltpu.SemaphoreType.DMA
    f32 = jnp.float32
    peers = gx_count * gy_count
    return pl.pallas_call(
        functools.partial(exchange_kernel, gx_count, gy_count, bool(held)),
        out_shape=[
            jax.ShapeDtypeStruct(e_right.shape, f32),
            jax.ShapeDtypeStruct(e_left.shape, f32),
            jax.ShapeDtypeStruct((gx_count,) + lo.shape, f32),
            jax.ShapeDtypeStruct((gx_count,) + hi.shape, f32),
            jax.ShapeDtypeStruct(mail.shape, f32),
        ] + [jax.ShapeDtypeStruct(h.shape, h.dtype) for h in held],
        in_specs=[vm] * 5 + [pl.BlockSpec(memory_space=pltpu.HBM)] * len(held),
        out_specs=[vm] * (5 + len(held)),
        scratch_shapes=[sem((2,)), sem((2,))] + [sem((gx_count,))] * 4 + [sem((peers,)), sem((peers,)), sem] + [sem] * len(held),
        compiler_params=pltpu.CompilerParams(
            collective_id=which, has_side_effects=True, vmem_limit_bytes=8 * MIB),
        name="exchange_%d" % which,
    )(e_right, e_left, lo, hi, mail, *held)


def column(count):
    peers = count.shape[1]
    return jnp.broadcast_to(count.astype(jnp.float32), (8, peers)).T[:, 0:1].astype(jnp.int32)


def put_ends(new, i, dims, e_right, e_left, lo, hi):
    nz, cy, cx = dims
    at = pl.ds(pl.multiple_of(i * 128, 128), 128)
    lanes = lax.broadcasted_iota(jnp.int32, (128, 128), 1)
    ends = pltpu.roll(jnp.where(lanes < 64, new[:, :128], new[:, cx - 128:]), 2, 1).T
    e_right[:, at] = ends[0:2]
    e_left[:, at] = ends[2:4]
    for k in range(128 // cy):
        z = i * (128 // cy) + k
        for row in range(2):
            lo[row, pl.ds(z, 1)] = new[k * cy + row:k * cy + row + 1]
            hi[row, pl.ds(z, 1)] = new[k * cy + cy - 2 + row:k * cy + cy - 1 + row]


def prepare_kernel(dims, f_at, cell_at, temp_at, coef_at, heat_at, count_at,
                   e_right, e_left, lo, hi, mail, f, cell, temp, coef, heat, count, sems):
    nz, cy, cx = dims
    pairs = ((cell_at, cell), (temp_at, temp), (coef_at, coef), (heat_at, heat), (count_at, count), (f_at, f))
    copies = [pltpu.make_async_copy(a, b, sems.at[k]) for k, (a, b) in enumerate(pairs)]
    for c in copies:
        c.start()
    for c in copies[:-1]:
        c.wait()
    slot = lax.broadcasted_iota(jnp.int32, coef.shape[1:], 1)
    live = jnp.where(slot < column(count[...]), coef[0], 0.0)
    mail[:, 0, :] = jnp.concatenate([cell[0].astype(jnp.float32), temp[0]], axis=1)
    mail[:, 1, :] = jnp.concatenate([live, heat[0]], axis=1)

    copies[-1].wait()

    def part(i, carry):
        put_ends(f[pl.ds(pl.multiple_of(i * 128, 128), 128)], i, dims, e_right, e_left, lo, hi)
        return carry

    lax.fori_loop(0, nz * cy // 128, part, 0)


def ends_shapes(dims):
    nz, cy, cx = dims
    return ([jax.ShapeDtypeStruct((2, nz * cy), jnp.float32)] * 2
            + [jax.ShapeDtypeStruct((2, nz, cx), jnp.float32)] * 2)


def prepare(dims, f, cell, temp, coef, heat, count):
    vm = pl.BlockSpec(memory_space=pltpu.VMEM)
    peers, cap = cell.shape[1:]
    return pl.pallas_call(
        functools.partial(prepare_kernel, dims),
        out_shape=ends_shapes(dims) + [
            jax.ShapeDtypeStruct((peers, 2, 2 * cap), jnp.float32),
            jax.ShapeDtypeStruct(f.shape, f.dtype)],
        in_specs=[pl.BlockSpec(memory_space=pltpu.HBM)] * 6,
        out_specs=[vm] * 6,
        scratch_shapes=[pltpu.VMEM(a.shape, a.dtype) for a in (cell, temp, coef, heat, count)]
        + [pltpu.SemaphoreType.DMA((6,))],
        compiler_params=pltpu.CompilerParams(vmem_limit_bytes=8 * MIB),
        name="prepare",
    )(f, cell, temp, coef, heat, count)


def plan(which, dims, shear, gx_count, gy_count):
    cx = dims[2]
    gx = lax.axis_index("gx")
    gy = lax.axis_index("gy")
    full_x = cx * gx_count
    offset = shear[which]
    up = lax.rem(gx * cx + full_x - jnp.where(gy == gy_count - 1, offset, 0), full_x)
    low = lax.rem(gx * cx + jnp.where(gy == 0, offset, 0), full_x)
    return lax.div(up, cx), lax.rem(up, cx), lax.div(low, cx), lax.rem(low, cx), gy


def stencil(dims, full_y, f, vel, o_left, o_right, y_up, y_low, info, xe, yg, ring, store):
    nz, cy, cx = dims
    gx_count = y_up.shape[0]
    k8 = lax.broadcasted_iota(jnp.int32, (8, 128), 0)
    l8 = lax.broadcasted_iota(jnp.int32, (8, 128), 1)
    hot = ((k8 == 0) & (l8 == 126)) | ((k8 == 1) & (l8 == 127)) | ((k8 == 2) & (l8 == 0)) | ((k8 == 3) & (l8 == 1))
    place = jnp.where(hot, 1.0, 0.0).astype(jnp.float32)
    edges = jnp.concatenate(
        [o_left[...], o_right[...], jnp.zeros((4, nz * cy), jnp.float32)], axis=0)
    xe[...] = lax.dot_general(
        edges, place, (((0,), (0,)), ((), ())), precision=lax.Precision.HIGHEST,
        preferred_element_type=jnp.float32)

    lane = lax.broadcasted_iota(jnp.int32, (nz, cx), 1)
    for src, q_at, base in ((y_up, 0, 0), (y_low, 2, 2)):
        q = info[q_at]
        rem = info[q_at + 1]
        nxt = lax.rem(q + 1, gx_count)
        turn = lax.rem(cx - rem, cx)
        for row in range(2):
            a = pltpu.roll(src[q, row], turn, 1)
            b = pltpu.roll(src[nxt, row], turn, 1)
            yg[base + row] = jnp.where(lane < cx - rem, a, b)

    start = (info[4] * cy).astype(jnp.float32)
    rows = lax.broadcasted_iota(jnp.int32, (cy, cx), 0).astype(jnp.float32) + start
    mean_flow = mean_speed * (2.0 * (rows + 0.5) * (1.0 / full_y) - 1.0)
    c8 = 8.0 / 12.0
    c1 = 1.0 / 12.0
    d16 = diffusivity * 16.0 / 12.0
    d1 = diffusivity / 12.0
    d30 = diffusivity * 90.0 / 12.0

    def plane(z, carry):
        c = f[pl.ds(pl.multiple_of(z * cy, cy), cy)]
        zm2 = f[pl.ds(pl.multiple_of(lax.rem(z + nz - 2, nz) * cy, cy), cy)]
        zm1 = f[pl.ds(pl.multiple_of(lax.rem(z + nz - 1, nz) * cy, cy), cy)]
        zp1 = f[pl.ds(pl.multiple_of(lax.rem(z + 1, nz) * cy, cy), cy)]
        zp2 = f[pl.ds(pl.multiple_of(lax.rem(z + 2, nz) * cy, cy), cy)]
        ring[0:cy] = c
        ring[cy:cy + 1] = yg[0, pl.ds(z, 1)]
        ring[cy + 1:cy + 2] = yg[1, pl.ds(z, 1)]
        ring[cy + 6:cy + 7] = yg[2, pl.ds(z, 1)]
        ring[cy + 7:cy + 8] = yg[3, pl.ds(z, 1)]
        ry = ring[...]
        ym2 = pltpu.roll(ry, 2, 0)[:cy]
        ym1 = pltpu.roll(ry, 1, 0)[:cy]
        yp1 = pltpu.roll(ry, cy + 7, 0)[:cy]
        yp2 = pltpu.roll(ry, cy + 6, 0)[:cy]
        rx = jnp.concatenate([c, xe[pl.ds(pl.multiple_of(z * cy, cy), cy)]], axis=1)
        wide = cx + 128
        xm2 = pltpu.roll(rx, 2, 1)[:, :cx]
        xm1 = pltpu.roll(rx, 1, 1)[:, :cx]
        xp1 = pltpu.roll(rx, wide - 1, 1)[:, :cx]
        xp2 = pltpu.roll(rx, wide - 2, 1)[:, :cx]
        u = vel[0, z].astype(jnp.float32) + mean_flow
        v = vel[1, z].astype(jnp.float32)
        w = vel[2, z].astype(jnp.float32)
        gx_ = c8 * (xp1 - xm1) - c1 * (xp2 - xm2)
        gy_ = c8 * (yp1 - ym1) - c1 * (yp2 - ym2)
        gz_ = c8 * (zp1 - zm1) - c1 * (zp2 - zm2)
        near = ((xp1 + xm1) + (yp1 + ym1)) + (zp1 + zm1)
        far = ((xp2 + xm2) + (yp2 + ym2)) + (zp2 + zm2)
        rhs = (d16 * near - d1 * far - d30 * c) - u * gx_ - v * (gy_ + mean_gradient) - w * gz_
        euler = c + time_step * rhs
        store(z, pl.ds(pl.multiple_of(z * cy, cy), cy), euler)
        return carry

    lax.fori_loop(0, nz, plane, 0, unroll=2)


def particles(second, rows, rt, now, nxt, field, accs, buf, peers):
    cap = buf.shape[1]
    scale = time_step * heat_share * (0.25 if second else 1.0)
    lane = lax.broadcasted_iota(jnp.int32, (cap, LANES), 1)
    src = lax.broadcasted_iota(jnp.int32, (cap, LANES), 1)

    def group(b, carry):
        s = b * GROUP
        turn = lax.rem(LANES - s, LANES)
        t = pltpu.roll(rt[...], turn, 1)
        old = pltpu.roll(now[...], turn, 1)
        made = nxt[...]
        for g in range(GROUP):
            for i in range(cap):
                buf[g, i:i + 1] = field[pl.ds(rows[s + g, i], 1)]
        for g in range(GROUP):
            hit = lane == t[0:cap, g:g + 1].astype(jnp.int32) % LANES
            sample = jnp.sum(jnp.where(hit, buf[g], 0.0), axis=1, keepdims=True)
            temp = old[:, g:g + 1]
            flux = t[2 * cap:3 * cap, g:g + 1] * (temp - sample)
            new = temp + time_step * (t[3 * cap:, g:g + 1] - flux)
            if second:
                new = 0.75 * t[cap:2 * cap, g:g + 1] + 0.25 * new
            made = jnp.where(src == s + g, new, made)
            buf[g] = jnp.where(hit, scale * flux, 0.0)
        nxt[...] = made
        for g in range(GROUP):
            for i in range(0, cap, WAYS):
                ats = [pl.ds(rows[s + g, i + k], 1) for k in range(WAYS)]
                adds = [accs[k][ats[k]] + buf[g, i + k:i + k + 1] for k in range(WAYS)]
                for k in range(WAYS):
                    accs[k][ats[k]] = adds[k]
        return carry

    lax.fori_loop(0, peers // GROUP, group, 0)


def first_kernel(dims, full_y, f, vel, o_left, o_right, y_up, y_low, came, shear, rows,
                 s1, q2, e_right, e_left, lo, hi, home,
                 xe, yg, ring, rt, t1, t2, buf, split, *accs):
    nz, cy, cx = dims
    peers = came.shape[0]
    cap = home.shape[2]
    zero = jnp.zeros((cy, LANES), jnp.float32)
    cells = nz * cy
    halves = [(h * cells, slice(h * LANES, (h + 1) * LANES)) for h in range(cx // LANES)]
    info = plan(0, dims, shear, y_up.shape[0], full_y // cy)

    def store(z, at, euler):
        for base, half in halves:
            to = pl.ds(pl.multiple_of(base + z * cy, cy), cy)
            split[to] = f[at, half]
            accs[0][to] = euler[:, half]
            for acc in accs[1:]:
                acc[to] = zero

    stencil(dims, full_y, f, vel, o_left, o_right, y_up, y_low, info, xe, yg, ring, store)
    for half in range(2):
        got = came[:, half, :]
        if peers < LANES:
            got = jnp.concatenate([got, jnp.zeros((LANES - peers, 2 * cap), jnp.float32)], axis=0)
        rt[2 * cap * half:2 * cap * (half + 1)] = got.T
    t1[...] = jnp.zeros_like(t1)
    t2[...] = jnp.zeros_like(t2)
    particles(False, rows, rt, rt.at[cap:2 * cap], t1, split, accs, buf, peers)

    def total_one(i, carry):
        at = pl.ds(pl.multiple_of(i * 128, 128), 128)
        news = []
        for base, half in halves:
            to = pl.ds(pl.multiple_of(base + i * 128, 128), 128)
            new = (accs[0][to] + accs[1][to]) + (accs[2][to] + accs[3][to])
            s1[at, half] = new
            split[to] = new
            for acc in accs:
                acc[to] = jnp.zeros_like(new)
            news.append(new)
        new = jnp.concatenate(news, axis=1)
        put_ends(new, i, dims, e_right, e_left, lo, hi)
        return carry

    lax.fori_loop(0, nz * cy // 128, total_one, 0)
    particles(True, rows, rt, t1, t2, split, accs, buf, peers)
    home[:, 0, :] = t2[...].T[:peers]

    def total_two(i, carry):
        at = pl.ds(pl.multiple_of(i * 64, 64), 64)
        for base, half in halves:
            to = pl.ds(pl.multiple_of(base + i * 64, 64), 64)
            q2[at, half] = (accs[0][to] + accs[1][to]) + (accs[2][to] + accs[3][to])
        return carry

    lax.fori_loop(0, nz * cy // 64, total_two, 0)


def work_space(dims):
    nz, cy, cx = dims
    f32 = jnp.float32
    return [pltpu.VMEM((nz * cy, 128), f32), pltpu.VMEM((4, nz, cx), f32), pltpu.VMEM((cy + 8, cx), f32)]


def first(dims, full_y, cap, f, vel, halos, came, info, rows):
    nz, cy, cx = dims
    f32 = jnp.float32
    vm = pl.BlockSpec(memory_space=pltpu.VMEM)
    sm = pl.BlockSpec(memory_space=pltpu.SMEM)
    grid = jax.ShapeDtypeStruct((nz * cy, cx), f32)
    space = pltpu.VMEM((nz * cy * (cx // LANES), LANES), f32)
    return pl.pallas_call(
        functools.partial(first_kernel, dims, full_y),
        out_shape=[grid, grid] + ends_shapes(dims) + [jax.ShapeDtypeStruct((came.shape[0], 1, cap), f32)],
        in_specs=[vm] * 7 + [sm, sm],
        out_specs=[vm] * 7,
        scratch_shapes=work_space(dims) + [
            pltpu.VMEM((4 * cap, LANES), f32), pltpu.VMEM((cap, LANES), f32), pltpu.VMEM((cap, LANES), f32),
            pltpu.VMEM((GROUP, cap, LANES), f32)] + [space] * 5,
        compiler_params=pltpu.CompilerParams(vmem_limit_bytes=26 * MIB),
        name="section_one",
    )(f, vel, *halos, came, info, rows)


def second_kernel(dims, full_y, f, vel, o_left, o_right, y_up, y_low, f0, q2, home, count, shear,
                  out, temp_out, xe, yg, ring):
    info = plan(1, dims, shear, y_up.shape[0], full_y // dims[1])

    def store(z, at, euler):
        out[z] = 0.75 * f0[at] + 0.25 * euler + q2[at]

    back = home[:, 0, :]
    slot = lax.broadcasted_iota(jnp.int32, back.shape, 1)
    temp_out[0] = jnp.where(slot < column(count[...]), back, 0.0)
    stencil(dims, full_y, f, vel, o_left, o_right, y_up, y_low, info, xe, yg, ring, store)


def second(dims, full_y, f, vel, halos, f0, q2, home, count, info):
    f32 = jnp.float32
    vm = pl.BlockSpec(memory_space=pltpu.VMEM)
    return pl.pallas_call(
        functools.partial(second_kernel, dims, full_y),
        out_shape=[jax.ShapeDtypeStruct(dims, f32),
                   jax.ShapeDtypeStruct((1, home.shape[0], home.shape[2]), f32)],
        in_specs=[vm] * 10 + [pl.BlockSpec(memory_space=pltpu.SMEM)],
        out_specs=[vm] * 2,
        scratch_shapes=work_space(dims),
        compiler_params=pltpu.CompilerParams(vmem_limit_bytes=26 * MIB),
        name="section_two",
    )(f, vel, *halos, f0, q2, home, count, info)


def on_device(
    scalar_field, velocity, shear_offset, part_temp, part_coef, part_heat, part_cell, part_count
):
    nz, cy, cx = scalar_field.shape
    cap = part_temp.shape[2]
    gx_count = lax.axis_size("gx")
    gy_count = lax.axis_size("gy")
    full_y = cy * gy_count
    dims = (nz, cy, cx)
    field = scalar_field.reshape(nz * cy, cx)

    *sends, near_field = prepare(dims, field, part_cell, part_temp, part_coef, part_heat, part_count)
    *halos, came, near = exchange(0, gx_count, gy_count, *sends, velocity)
    cells = came[:, 0, :cap].astype(jnp.int32)
    rows = cells % cx // LANES * (nz * cy) + cells // cx
    section_one, source, *sends = first(
        dims, full_y, cap, near_field, near, halos, came, shear_offset, rows)
    *halos, home = exchange(1, gx_count, gy_count, *sends)
    scalar_out, temp_out = second(
        dims, full_y, section_one, near, halos, near_field, source, home, part_count,
        shear_offset)
    return (scalar_out, temp_out)


def solution(mesh):
    in_specs = (
        P(None, "gy", "gx"),
        P(None, None, "gy", "gx"),
        P(),
        P(("gx", "gy"), None, None),
        P(("gx", "gy"), None, None),
        P(("gx", "gy"), None, None),
        P(("gx", "gy"), None, None),
        P(("gx", "gy"), None),
    )
    out_specs = (P(None, "gy", "gx"), P(("gx", "gy"), None, None))
    return jax.shard_map(
        on_device, mesh=mesh, in_specs=in_specs, out_specs=out_specs, check_vma=False
    )
```
